512 devices in a mesh: sec: 32 (over x, y), head: 16 (over z, core).
Axes of the slice: x: 4, y: 8, z: 8, core: 2. Of those that a mesh axis runs over, the one named last changes fastest.
Arguments:
- tokens: bfloat16 [32768, 2048], P('sec', 'head'), may hold values from -6 to 6
- fresh_tokens: bfloat16 [1024, 2048], P(None, 'head'), may hold values from -6 to 6
- route_rows: int32 [32, 4, 128], P('sec'), may hold values from 0 to 255, as said below
- block_list: int32 [32, 4, 16], P('sec'), may hold values from 0 to 31, all different within a row
- norm_gain: float32 [32, 2048], P('sec'), may hold values from 0.25 to 1.75
- route_weight: bfloat16 [32, 2048], P('sec'), may hold values from -0.125 to 0.125
- w_query: bfloat16 [32, 2048, 2048], P('sec', None, 'head'), may hold values from -0.125 to 0.125
- w_key: bfloat16 [32, 2048, 2048], P('sec', None, 'head'), may hold values from -0.26367188 to 0.26367188
- w_value: bfloat16 [32, 2048, 2048], P('sec', None, 'head'), may hold values from -0.125 to 0.125
- w_out: bfloat16 [32, 2048, 2048], P('sec', None, 'head'), may hold values from -0.52734375 to 0.52734375
- cache_keys: bfloat16 [32, 4096, 2048], P('sec', None, 'head'), may hold values from -2400 to 2400
- cache_values: bfloat16 [32, 4096, 2048], P('sec', None, 'head'), may hold values from -6 to 6
Outputs:
- next_input: bfloat16 [32768, 2048], P('sec', 'head')
The draws below stay inside these ranges and needn't reach their ends.
Inputs may be any that keep to these rules, and one draw needn't show every extreme that they name: `route_rows`: within one section and group the 128 entries are distinct row numbers of the group. `block_list`: each section's group names 16 distinct blocks.
All inputs are finite; a program needn't handle non-finite values.
Results may differ from the reference program's by a relative error of at most 0.017.
Values may be sent and summed in bfloat16 or wider, within the bound.
A program may use at most 64 MiB of HBM per device.

```python
import math
import jax
import jax.numpy as jnp
from jax import lax

D = 2048
HEADS = 32
HEAD_DIM = 64
GROUP = 256
GROUPS = 4
CACHE = 4096
BLOCK = 128
TOK_DEV = 1024
ROUTED_GROUP = 128
CACHE_BLOCKS = 32
PICKED = 16
TOKENS = 32768
N_SEC = 32


def draw_route_rows(key, part):
    row_keys = jax.random.split(jax.random.fold_in(key, 11), N_SEC * GROUPS)
    chosen = jax.vmap(lambda one_key: jax.random.permutation(one_key, GROUP)[:ROUTED_GROUP])(row_keys)
    return chosen.reshape(N_SEC, GROUPS, ROUTED_GROUP).astype(jnp.int32)


def draw_cache_keys(key, part):
    first = jax.random.fold_in(jax.random.fold_in(key, 23), 0)
    shape = (N_SEC, CACHE, HEADS, HEAD_DIM)
    base = jnp.clip(jax.random.normal(first, shape, jnp.float32), -8.0, 8.0) * 2.0
    return base.reshape(N_SEC, CACHE, HEADS * HEAD_DIM).astype(jnp.bfloat16)


def block_scale(stream_key, shape, pieces, smallest, high):
    loudness = 1.0
    for position, parts in pieces:
        steps = jax.random.uniform(jax.random.fold_in(jax.random.fold_in(stream_key, 6), position), (parts,), jnp.float32, smallest / len(pieces), high / len(pieces))
        loudness = loudness * jnp.repeat(jnp.exp(steps), shape[position] // parts).reshape((-1,) + (1,) * (len(shape) - 1 - position))
    return loudness


def choose_distinct(key, rows, number_of, top, lift):
    sequence = jax.random.permutation(jax.random.fold_in(key, 1), number_of)
    pull = sequence
    for power in range(3):
        pull = pull * pull // number_of
    pull = pull * lift // number_of
    chance = jax.random.randint(jax.random.fold_in(key, 2), (rows, number_of), 0, 4096) + pull
    fixed_rows = jax.random.permutation(jax.random.fold_in(key, 3), rows)[jnp.arange(number_of) % rows]
    chance = jnp.where(jnp.arange(rows)[:, None] == fixed_rows[None, :], 1 << 14, chance)
    priority = chance * number_of + jnp.arange(number_of)
    return lax.top_k(priority.astype(jnp.int32), top)[1].astype(jnp.int32)


def gaussian(key, shape, deviation, most, pieces=(), kind=jnp.bfloat16):
    array = jax.random.normal(key, shape, jnp.float32) * deviation
    if len(pieces) > 0:
        array = block_scale(key, shape, pieces, -0.22, 0.18) * array
    return jnp.clip(array, min=-most, max=most).astype(kind)


def setup_inputs(seed: int = 0) -> dict:
    splits = jax.random.split(jax.random.key(seed), 13)
    tokens = gaussian(splits[0], (TOKENS, D), 1.0, 6.0, ((0, 32), (1, 16)))
    fresh_tokens = gaussian(splits[1], (TOK_DEV, D), 1.0, 6.0, ((1, 16),))
    route_rows = draw_route_rows(jax.random.fold_in(splits[12], 71), 0)
    block_list = choose_distinct(splits[3], N_SEC * GROUPS, CACHE_BLOCKS, PICKED, 0).reshape((N_SEC, GROUPS, PICKED))
    norm_gain = jnp.clip(1.0 + 0.15 * jax.random.normal(splits[4], (N_SEC, D), jnp.float32), 0.25, 1.75)
    route_weight = gaussian(splits[5], (N_SEC, D), D ** -0.5, 0.125, ((0, 32),))
    w_query = gaussian(splits[6], (N_SEC, D, HEADS * HEAD_DIM), D ** -0.5, 0.125, ((0, 32), (2, 16)))
    w_key = gaussian(splits[7], (N_SEC, D, HEADS * HEAD_DIM), (2.0 / D ** 0.5), 0.26367188, ((0, 32), (2, 16)))
    w_value = gaussian(splits[8], (N_SEC, D, HEADS * HEAD_DIM), D ** -0.5, 0.125, ((0, 32), (2, 16)))
    w_out = gaussian(splits[9], (N_SEC, HEADS * HEAD_DIM, D), (4.0 / (HEADS * HEAD_DIM) ** 0.5), 0.52734375, ((0, 32), (2, 16)))
    cache_keys = draw_cache_keys(jax.random.fold_in(splits[12], 71), 0)
    cache_values = gaussian(splits[11], (N_SEC, CACHE, HEADS * HEAD_DIM), 1.0, 6.0, ((0, 32), (2, 16)))
    return dict(tokens=tokens, fresh_tokens=fresh_tokens, route_rows=route_rows, block_list=block_list, norm_gain=norm_gain, route_weight=route_weight, w_query=w_query, w_key=w_key, w_value=w_value, w_out=w_out, cache_keys=cache_keys, cache_values=cache_values)


def attend_all(queries, key_rows, value_rows, row_index, cache_k, cache_v, picks):
    row_count, head_count, head_width = queries.shape
    group_count = picks.shape[0]
    score_scale = 1.0 / math.sqrt(head_width)
    chosen_keys = cache_k.reshape(-1, BLOCK, head_count, head_width)[picks].reshape(group_count, -1, head_count, head_width)
    chosen_values = cache_v.reshape(-1, BLOCK, head_count, head_width)[picks].reshape(group_count, -1, head_count, head_width)
    query_groups = queries.reshape(group_count, -1, head_count, head_width)
    cache_scores = jnp.einsum('crhd,ckhd->chrk', query_groups.astype(jnp.float32), chosen_keys.astype(jnp.float32)) * score_scale
    local_scores = jnp.einsum('qhd,khd->hqk', queries.astype(jnp.float32), key_rows.astype(jnp.float32)) * score_scale
    visible = row_index[None, :] <= row_index[:, None]
    local_scores = jnp.where(visible[None], local_scores, -jnp.inf)
    cache_max = jnp.transpose(lax.optimization_barrier(jnp.max(cache_scores, axis=-1)), (1, 0, 2)).reshape(head_count, row_count)
    row_max = jnp.maximum(cache_max, lax.optimization_barrier(jnp.max(local_scores, axis=-1)))
    group_max = jnp.transpose(row_max.reshape(head_count, group_count, -1), (1, 0, 2))
    cache_weights = jnp.exp(cache_scores - group_max[..., None])
    local_weights = jnp.exp(local_scores - row_max[..., None])
    cache_sum = jnp.transpose(lax.optimization_barrier(jnp.sum(cache_weights, axis=-1)), (1, 0, 2)).reshape(head_count, row_count)
    denom_sum = cache_sum + lax.optimization_barrier(jnp.sum(local_weights, axis=-1))
    cache_probs = cache_weights.astype(jnp.bfloat16).astype(jnp.float32)
    local_probs = local_weights.astype(jnp.bfloat16).astype(jnp.float32)
    from_cache = jnp.einsum('chrk,ckhd->crhd', cache_probs, chosen_values.astype(jnp.float32)).reshape(row_count, head_count, head_width)
    from_local = jnp.einsum('hqk,khd->qhd', local_probs, value_rows.astype(jnp.float32))
    attended = (from_cache + from_local) / jnp.transpose(denom_sum)[:, :, None]
    return attended.astype(jnp.bfloat16).reshape(row_count, head_count * head_width)

def section(operands):
    rows_in, chosen, picks, gain_row, router, query_w, key_w, value_w, output_w, cache_k, cache_v = operands
    row_index = (chosen + GROUP * jnp.arange(GROUPS, dtype=jnp.int32)[:, None]).reshape(-1).astype(jnp.int32)
    picked = rows_in[row_index].astype(jnp.float32)
    mean_square = lax.optimization_barrier(jnp.mean(picked * picked, axis=-1, keepdims=True))
    normed = (picked * lax.rsqrt(mean_square + 1e-05) * gain_row[None, :]).astype(jnp.bfloat16)
    gate_value = jax.nn.sigmoid(jnp.dot(normed, router, preferred_element_type=jnp.float32))
    queries = jnp.dot(normed, query_w, preferred_element_type=jnp.float32).astype(jnp.bfloat16).reshape(-1, HEADS, HEAD_DIM)
    key_rows = jnp.dot(normed, key_w, preferred_element_type=jnp.float32).astype(jnp.bfloat16).reshape(-1, HEADS, HEAD_DIM)
    value_rows = jnp.dot(normed, value_w, preferred_element_type=jnp.float32).astype(jnp.bfloat16).reshape(-1, HEADS, HEAD_DIM)
    attended = attend_all(queries, key_rows, value_rows, row_index, cache_k, cache_v, picks)
    branch = jnp.dot(attended, output_w, preferred_element_type=jnp.float32)
    updated = (picked + gate_value[:, None] * branch).astype(jnp.bfloat16)
    return rows_in.at[row_index].set(updated)

def reference(tokens, fresh_tokens, route_rows, block_list, norm_gain, route_weight, w_query, w_key, w_value, w_out, cache_keys, cache_values):
    stacked = tokens.reshape(N_SEC, TOK_DEV, D)
    results = lax.map(section, (stacked, route_rows, block_list, norm_gain, route_weight, w_query, w_key, w_value, w_out, cache_keys, cache_values))
    shifted = jnp.concatenate([fresh_tokens[None], results[:-1]], axis=0)
    return shifted.reshape(TOKENS, D)
```

```python
import functools

import jax
import jax.numpy as jnp
from jax import lax
from jax.experimental import pallas as pl
from jax.experimental.pallas import tpu as pltpu
from jax.sharding import PartitionSpec as P

HEAD_DIM = 64
BLOCK = 128
WIDTH = 128
MESH = pl.DeviceIdType.MESH
F32 = jnp.float32
BF16 = jnp.bfloat16


def dot(a, b, dims=((1,), (0,))):
    return lax.dot_general(a, b, (dims, ((), ())), preferred_element_type=F32)


def kernel(
    sections,
    chips,
    blocks_ref,
    route_hbm,
    gain_hbm,
    router_hbm,
    tokens_hbm,
    wq_hbm,
    wk_hbm,
    wv_hbm,
    wo_hbm,
    ck_hbm,
    cv_hbm,
    out_ref,
    route,
    gain,
    router,
    tokens,
    wcat,
    wo,
    ck,
    cv,
    xg,
    ag,
    normed,
    scores,
    klocal,
    vlocal,
    gates,
    place,
    passed,
    result,
    load_sem,
    ring_send,
    ring_recv,
    pair_send,
    pair_recv,
    next_send,
    next_recv,
):
    groups, routed = route.shape
    group_rows = tokens.shape[0] // groups
    half = chips // 2
    picked_blocks = blocks_ref.shape[1]
    shards = 2 * chips
    width = shards * WIDTH

    sec = lax.axis_index("sec")
    head = lax.axis_index("head")
    chip = head // 2
    core = head % 2
    up = ((chip + 1) % chips) * 2 + core
    down = ((chip + chips - 1) % chips) * 2 + core
    pair = chip * 2 + 1 - core
    after = (sec + 1) % sections
    before = (sec + sections - 1) % sections

    loads = [
        pltpu.make_async_copy(a, b, load_sem.at[i])
        for i, (a, b) in enumerate(
            (
                (route_hbm, route),
                (tokens_hbm, tokens),
                (router_hbm, router),
                (gain_hbm, gain),
                (wq_hbm, wcat.at[:, pl.ds(0, WIDTH)]),
                (wk_hbm, wcat.at[:, pl.ds(WIDTH, WIDTH)]),
                (wv_hbm, wcat.at[:, pl.ds(2 * WIDTH, WIDTH)]),
                (ck_hbm, ck),
                (cv_hbm, cv),
                (wo_hbm, wo),
            )
        )
    ]
    for load in loads:
        load.start()

    barrier = pltpu.get_barrier_semaphore()
    for there in (
        {"head": up},
        {"head": down},
        {"head": pair},
        {"sec": after},
        {"sec": before},
    ):
        pl.semaphore_signal(barrier, inc=1, device_id=there, device_id_type=MESH)

    bufs = (xg, ag)

    def ring_copy(p, g, slot, hop, way):
        ref = bufs[p].at[g, slot]
        if hop == half:
            ref = ref.at[pl.ds(way * (routed // 2), routed // 2)]
        i = 2 * (hop - 1) + way
        return pltpu.make_async_remote_copy(
            src_ref=ref,
            dst_ref=ref,
            send_sem=ring_send.at[p, g, i],
            recv_sem=ring_recv.at[p, g, i],
            device_id={"head": up if way == 0 else down},
            device_id_type=MESH,
        )

    def pair_copy(p, g, slot, i):
        ref = bufs[p].at[g, slot]
        return pltpu.make_async_remote_copy(
            src_ref=ref,
            dst_ref=ref,
            send_sem=pair_send.at[p, g, i],
            recv_sem=pair_recv.at[p, g, i],
            device_id={"head": pair},
            device_id_type=MESH,
        )

    def arrived(hop, way):
        off = chips - hop if way == 0 else hop
        return ((chip + off) % chips) * 2 + core

    def send_own(p, g):
        for way in (0, 1):
            ring_copy(p, g, head, 1, way).start()
        pair_copy(p, g, head, 0).start()

    def ring_step(p, g, hop):
        for way in (0, 1):
            slot = arrived(hop, way)
            ring_copy(p, g, slot, hop, way).wait_recv()
            if hop < half:
                ring_copy(p, g, slot, hop + 1, way).start()
                pair_copy(p, g, slot, 2 * hop - 1 + way).start()
        if hop == half:
            pair_copy(p, g, arrived(hop, 0), 2 * half - 1).start()

    def pair_wait(p, g):
        for i in range(2 * half):
            pair_copy(p, g, pair, i).wait_recv()

    def drain(p, g):
        for hop in range(1, half + 1):
            for way in (0, 1):
                ring_copy(p, g, head, hop, way).wait_send()
        for i in range(2 * half):
            pair_copy(p, g, head, i).wait_send()

    def next_copy(g):
        return pltpu.make_async_remote_copy(
            src_ref=result.at[pl.ds(g * group_rows, group_rows)],
            dst_ref=out_ref.at[pl.ds(g * group_rows, group_rows)],
            send_sem=next_send.at[g],
            recv_sem=next_recv.at[g],
            device_id={"sec": after},
            device_id_type=MESH,
        )

    def pick(g):
        chosen = route[g : g + 1, :]
        rows = lax.broadcasted_iota(jnp.int32, (group_rows, routed), 0)
        one_hot = jnp.where(rows == chosen, 1.0, 0.0).astype(F32)
        here = one_hot.astype(BF16)
        place[g] = here
        mine = tokens[pl.ds(g * group_rows, group_rows), :]
        xg[g, head] = dot(here, mine, ((0,), (0,))).astype(BF16)
        used = jnp.max(one_hot, axis=1, keepdims=True)
        passed[pl.ds(g * group_rows, group_rows), :] = jnp.where(
            used > 0.0, 0.0, mine.astype(F32)
        ).astype(BF16)

    def project(g):
        total = jnp.zeros((routed, WIDTH), F32)
        for s in range(shards):
            x = xg[g, s].astype(F32)
            total += x * x
        mean = jnp.sum(total, axis=1, keepdims=True) * (1.0 / width)
        scale = lax.rsqrt(mean + 1e-05)
        for s in range(shards):
            lanes = slice(s * WIDTH, (s + 1) * WIDTH)
            x = xg[g, s].astype(F32)
            normed[:, lanes] = (x * scale * gain[:, lanes]).astype(BF16)
        y = dot(normed[...], wcat[...])
        gates[g] = jax.nn.sigmoid(y[:, 3 * WIDTH :])
        klocal[g] = y[:, WIDTH : 2 * WIDTH].astype(BF16)
        vlocal[g] = y[:, 2 * WIDTH : 3 * WIDTH].astype(BF16)
        return y[:, :WIDTH].astype(BF16)

    def attend(g, q):
        lane = lax.broadcasted_iota(jnp.int32, (routed, WIDTH), 1)
        first = lane < HEAD_DIM
        qs = q.astype(F32) * 0.125
        both = jnp.concatenate(
            [jnp.where(first, qs, 0.0), jnp.where(first, 0.0, qs)], axis=0
        ).astype(BF16)
        starts = [blocks_ref[g, i] for i in range(picked_blocks)]
        kinds = [(ck, cv, s) for s in starts] + [(klocal, vlocal, c) for c in range(g + 1)]

        r = jnp.broadcast_to(route[g : g + 1, :].astype(F32), (routed, routed))
        visible = r <= jnp.transpose(r)
        visible = jnp.concatenate([visible, visible], axis=0)
        spans = [kinds[i : i + 2] for i in range(0, len(kinds), 2)]
        top = None
        at = 0
        where = []
        for span in spans:
            keys = jnp.concatenate([k[i] for k, _, i in span], axis=0)
            s = dot(both, keys, ((1,), (1,)))
            for j, (k, _, i) in enumerate(span):
                part = s[:, j * BLOCK : (j + 1) * BLOCK]
                if k is klocal and i == g:
                    part = jnp.where(visible, part, -jnp.inf)
                scores[:, at + j * BLOCK : at + (j + 1) * BLOCK] = part
                top = part if top is None else jnp.maximum(top, part)
            where.append((at, BLOCK * len(span)))
            at += BLOCK * len(span)
        high = jnp.max(top, axis=1, keepdims=True)
        total = jnp.zeros((2 * routed, WIDTH), F32)
        acc = jnp.zeros((2 * routed, WIDTH), F32)
        for (at, size), span in zip(where, spans):
            w = jnp.exp(scores[:, at : at + size] - high)
            for j in range(len(span)):
                total += w[:, j * BLOCK : (j + 1) * BLOCK]
            values = jnp.concatenate([v[i] for _, v, i in span], axis=0)
            acc += dot(w.astype(BF16), values)
        denom = jnp.sum(total, axis=1, keepdims=True)
        ratio = acc / denom
        ag[g, head] = jnp.where(first, ratio[:routed], ratio[routed:]).astype(BF16)

    def finish(g):
        attended = jnp.concatenate([ag[g, s] for s in range(shards)], axis=1)
        branch = dot(attended, wo[...])
        updated = (xg[g, head].astype(F32) + gates[g] * branch).astype(BF16)
        rows = pl.ds(g * group_rows, group_rows)
        moved = dot(place[g], updated)
        result[rows, :] = (moved + passed[rows, :].astype(F32)).astype(BF16)
        next_copy(g).start()

    loads[0].wait()
    loads[1].wait()
    for g in range(groups):
        pick(g)
    pl.semaphore_wait(barrier, 5)
    for g in range(groups):
        send_own(0, g)

    loads[2].wait()
    for s in range(shards):
        lanes = slice(s * WIDTH, (s + 1) * WIDTH)
        wide = jnp.broadcast_to(router[:, lanes].astype(F32), (WIDTH, WIDTH))
        wcat[lanes, 3 * WIDTH :] = jnp.transpose(wide).astype(BF16)

    for hop in range(1, half + 1):
        for g in range(groups):
            ring_step(0, g, hop)
    for load in loads[3:]:
        load.wait()

    for t in range(groups + half):
        if t < groups:
            pair_wait(0, t)
            attend(t, project(t))
            send_own(1, t)
        for g in range(groups):
            if 1 <= t - g <= half:
                ring_step(1, g, t - g)
        done = t - half
        if done >= 0:
            pair_wait(1, done)
            finish(done)

    for g in range(groups):
        drain(0, g)
        drain(1, g)
        next_copy(g).wait()


def body(
    tokens,
    fresh_tokens,
    route_rows,
    block_list,
    norm_gain,
    route_weight,
    w_query,
    w_key,
    w_value,
    w_out,
    cache_keys,
    cache_values,
):
    sections = lax.axis_size("sec")
    shards = lax.axis_size("head")
    chips = shards // 2
    half = chips // 2
    groups, routed = route_rows.shape[1:]
    rows = tokens.shape[0]
    width = shards * WIDTH
    cached = cache_keys.shape[1] // BLOCK
    picked = block_list.shape[2] * BLOCK
    dma = pltpu.SemaphoreType.DMA
    hbm = pl.BlockSpec(memory_space=pl.ANY)
    shifted = pl.pallas_call(
        functools.partial(kernel, sections, chips),
        out_shape=jax.ShapeDtypeStruct((rows, WIDTH), BF16),
        in_specs=[pl.BlockSpec(memory_space=pltpu.SMEM)] + [hbm] * 10,
        out_specs=hbm,
        scratch_shapes=[
            pltpu.VMEM((groups, routed), jnp.int32),
            pltpu.VMEM((1, width), F32),
            pltpu.VMEM((1, width), BF16),
            pltpu.VMEM((rows, WIDTH), BF16),
            pltpu.VMEM((width, 4 * WIDTH), BF16),
            pltpu.VMEM((width, WIDTH), BF16),
            pltpu.VMEM((cached, BLOCK, WIDTH), BF16),
            pltpu.VMEM((cached, BLOCK, WIDTH), BF16),
            pltpu.VMEM((groups, shards, routed, WIDTH), BF16),
            pltpu.VMEM((groups, shards, routed, WIDTH), BF16),
            pltpu.VMEM((routed, width), BF16),
            pltpu.VMEM((2 * routed, picked + groups * routed), F32),
            pltpu.VMEM((groups, routed, WIDTH), BF16),
            pltpu.VMEM((groups, routed, WIDTH), BF16),
            pltpu.VMEM((groups, routed, WIDTH), F32),
            pltpu.VMEM((groups, rows // groups, routed), BF16),
            pltpu.VMEM((rows, WIDTH), BF16),
            pltpu.VMEM((rows, WIDTH), BF16),
            dma((10,)),
            dma((2, groups, 2 * half)),
            dma((2, groups, 2 * half)),
            dma((2, groups, 2 * half)),
            dma((2, groups, 2 * half)),
            dma((groups,)),
            dma((groups,)),
        ],
        compiler_params=pltpu.CompilerParams(
            collective_id=0, has_side_effects=True, vmem_limit_bytes=60 << 20
        ),
    )(
        block_list[0],
        route_rows[0],
        norm_gain,
        route_weight,
        tokens,
        w_query[0],
        w_key[0],
        w_value[0],
        w_out[0],
        cache_keys[0].reshape(cached, BLOCK, WIDTH),
        cache_values[0].reshape(cached, BLOCK, WIDTH),
    )
    return jnp.where(lax.axis_index("sec") == 0, fresh_tokens, shifted)


def solution(mesh):
    in_specs = (
        P("sec", "head"),
        P(None, "head"),
        P("sec", None, None),
        P("sec", None, None),
        P("sec", None),
        P("sec", None),
        P("sec", None, "head"),
        P("sec", None, "head"),
        P("sec", None, "head"),
        P("sec", None, "head"),
        P("sec", None, "head"),
        P("sec", None, "head"),
    )
    return jax.shard_map(
        body, mesh=mesh, in_specs=in_specs, out_specs=P("sec", "head"), check_vma=False
    )
```

```python
import functools

import jax
import jax.numpy as jnp
from jax import lax
from jax.experimental import pallas as pl
from jax.experimental.pallas import tpu as pltpu
from jax.sharding import PartitionSpec as P

HEAD_DIM = 64
BLOCK = 128
WIDTH = 128
MESH = pl.DeviceIdType.MESH
OWN = ((1,), (1, 2))
ONWARD = ({1: (2,), 2: (3, 4)}, {2: (3, 4)})
F32 = jnp.float32
BF16 = jnp.bfloat16


def dot(a, b, dims=((1,), (0,))):
    return lax.dot_general(a, b, (dims, ((), ())), preferred_element_type=F32)


def kernel(
    sections,
    chips,
    blocks_ref,
    route_hbm,
    gain_hbm,
    router_hbm,
    tokens_hbm,
    wq_hbm,
    wk_hbm,
    wv_hbm,
    wo_hbm,
    ck_hbm,
    cv_hbm,
    out_ref,
    route,
    gain,
    router,
    tokens,
    wcat,
    wo,
    ck,
    cv,
    xg,
    ag,
    normed,
    scores,
    klocal,
    vlocal,
    gates,
    place,
    passed,
    result,
    load_sem,
    ring_send,
    ring_recv,
    pair_send,
    pair_recv,
    next_send,
    next_recv,
):
    groups, routed = route.shape
    group_rows = tokens.shape[0] // groups
    half = chips // 2
    picked_blocks = blocks_ref.shape[1]
    shards = 2 * chips
    width = shards * WIDTH

    sec = lax.axis_index("sec")
    head = lax.axis_index("head")
    chip = head // 2
    core = head % 2

    def at(off):
        return ((chip + chips + off) % chips) * 2 + core

    pair = chip * 2 + 1 - core
    after = (sec + 1) % sections
    before = (sec + sections - 1) % sections

    def rows_of(g):
        return pl.ds(g * group_rows, group_rows)

    def load(i, source, target):
        copy = pltpu.make_async_copy(source, target, load_sem.at[i])
        copy.start()
        return copy

    route_load = load(0, route_hbm, route)
    token_loads = [
        load(1 + g, tokens_hbm.at[rows_of(g)], tokens.at[rows_of(g)])
        for g in range(groups)
    ]

    barrier = pltpu.get_barrier_semaphore()
    for there in (
        {"head": at(1)},
        {"head": at(-1)},
        {"head": at(2)},
        {"head": at(-2)},
        {"head": pair},
        {"sec": after},
        {"sec": before},
    ):
        pl.semaphore_signal(barrier, inc=1, device_id=there, device_id_type=MESH)

    bufs = (xg, ag)

    def message(p, g, way, reach, dist, slot):
        ref = bufs[p].at[g, slot]
        if reach == half:
            ref = ref.at[pl.ds(way * (routed // 2), routed // 2)]
        i = 2 * (reach - 1) + way
        return pltpu.make_async_remote_copy(
            src_ref=ref,
            dst_ref=ref,
            send_sem=ring_send.at[p, g, i],
            recv_sem=ring_recv.at[p, g, i],
            device_id={"head": at(dist if way == 0 else -dist)},
            device_id_type=MESH,
        )

    def pair_copy(p, g, slot, i):
        ref = bufs[p].at[g, slot]
        return pltpu.make_async_remote_copy(
            src_ref=ref,
            dst_ref=ref,
            send_sem=pair_send.at[p, g, i],
            recv_sem=pair_recv.at[p, g, i],
            device_id={"head": pair},
            device_id_type=MESH,
        )

    def arrived(reach, way):
        return at(-reach if way == 0 else reach)

    def send_own(p, g):
        for reach in OWN[p]:
            for way in (0, 1):
                message(p, g, way, reach, reach, head).start()
        pair_copy(p, g, head, 0).start()

    def step(p, g, reach):
        for way in (0, 1):
            slot = arrived(reach, way)
            message(p, g, way, reach, 1, slot).wait_recv()
            for farther in ONWARD[p].get(reach, ()):
                message(p, g, way, farther, farther - reach, slot).start()
            if reach < half:
                pair_copy(p, g, slot, 2 * reach - 1 + way).start()
        if reach == half:
            pair_copy(p, g, arrived(reach, 0), 2 * half - 1).start()

    def steps(p, g, *reaches):
        for reach in reaches:
            step(p, g, reach)

    def pair_wait(p, g):
        for i in range(2 * half):
            pair_copy(p, g, pair, i).wait_recv()

    def drain(p, g):
        for reach in range(1, half + 1):
            for way in (0, 1):
                message(p, g, way, reach, 1, head).wait_send()
        for i in range(2 * half):
            pair_copy(p, g, head, i).wait_send()

    def next_copy(g):
        return pltpu.make_async_remote_copy(
            src_ref=result.at[rows_of(g)],
            dst_ref=out_ref.at[rows_of(g)],
            send_sem=next_send.at[g],
            recv_sem=next_recv.at[g],
            device_id={"sec": after},
            device_id_type=MESH,
        )

    def pick(g):
        chosen = route[g : g + 1, :]
        rows = lax.broadcasted_iota(jnp.int32, (group_rows, routed), 0)
        here = jnp.where(rows == chosen, 1.0, 0.0).astype(BF16)
        place[g] = here
        token_loads[g].wait()
        xg[g, head] = dot(here, tokens[rows_of(g), :], ((0,), (0,))).astype(BF16)

    def pass_rest(g):
        used = jnp.max(place[g].astype(F32), axis=1, keepdims=True)
        mine = tokens[rows_of(g), :].astype(F32)
        passed[rows_of(g), :] = jnp.where(used > 0.0, 0.0, mine).astype(BF16)

    def project(g):
        total = jnp.zeros((routed, WIDTH), F32)
        for s in range(shards):
            x = xg[g, s].astype(F32)
            total += x * x
        mean = jnp.sum(total, axis=1, keepdims=True) * (1.0 / width)
        scale = lax.rsqrt(mean + 1e-05)
        for s in range(shards):
            lanes = slice(s * WIDTH, (s + 1) * WIDTH)
            x = xg[g, s].astype(F32)
            normed[:, lanes] = (x * scale * gain[:, lanes]).astype(BF16)
        y = dot(normed[...], wcat[...])
        gates[g] = jax.nn.sigmoid(y[:, 3 * WIDTH :])
        klocal[g] = y[:, WIDTH : 2 * WIDTH].astype(BF16)
        vlocal[g] = y[:, 2 * WIDTH : 3 * WIDTH].astype(BF16)
        return y[:, :WIDTH].astype(BF16)

    def attend(g, q):
        lane = lax.broadcasted_iota(jnp.int32, (routed, WIDTH), 1)
        first = lane < HEAD_DIM
        qs = q.astype(F32) * 0.125
        both = jnp.concatenate(
            [jnp.where(first, qs, 0.0), jnp.where(first, 0.0, qs)], axis=0
        ).astype(BF16)
        starts = [blocks_ref[g, i] for i in range(picked_blocks)]
        kinds = [(ck, cv, s) for s in starts] + [(klocal, vlocal, c) for c in range(g + 1)]

        r = jnp.broadcast_to(route[g : g + 1, :].astype(F32), (routed, routed))
        visible = r <= jnp.transpose(r)
        visible = jnp.concatenate([visible, visible], axis=0)
        spans = [kinds[i : i + 2] for i in range(0, len(kinds), 2)]
        top = None
        at = 0
        where = []
        for span in spans:
            keys = jnp.concatenate([k[i] for k, _, i in span], axis=0)
            s = dot(both, keys, ((1,), (1,)))
            for j, (k, _, i) in enumerate(span):
                part = s[:, j * BLOCK : (j + 1) * BLOCK]
                if k is klocal and i == g:
                    part = jnp.where(visible, part, -jnp.inf)
                scores[:, at + j * BLOCK : at + (j + 1) * BLOCK] = part
                top = part if top is None else jnp.maximum(top, part)
            where.append((at, BLOCK * len(span)))
            at += BLOCK * len(span)
        high = jnp.max(top, axis=1, keepdims=True)
        total = jnp.zeros((2 * routed, WIDTH), F32)
        acc = jnp.zeros((2 * routed, WIDTH), F32)
        for (at, size), span in zip(where, spans):
            w = jnp.exp(scores[:, at : at + size] - high)
            for j in range(len(span)):
                total += w[:, j * BLOCK : (j + 1) * BLOCK]
            values = jnp.concatenate([v[i] for _, v, i in span], axis=0)
            acc += dot(w.astype(BF16), values)
        denom = jnp.sum(total, axis=1, keepdims=True)
        ratio = acc / denom
        ag[g, head] = jnp.where(first, ratio[:routed], ratio[routed:]).astype(BF16)

    def finish(g):
        pair_wait(1, g)
        attended = jnp.concatenate([ag[g, s] for s in range(shards)], axis=1)
        branch = dot(attended, wo[...])
        updated = (xg[g, head].astype(F32) + gates[g] * branch).astype(BF16)
        moved = dot(place[g], updated)
        rest = passed[rows_of(g), :].astype(F32)
        result[rows_of(g), :] = (moved + rest).astype(BF16)
        next_copy(g).start()

    def compute(g):
        pair_wait(0, g)
        attend(g, project(g))
        send_own(1, g)

    route_load.wait()
    pick(0)
    pl.semaphore_wait(barrier, 7)
    send_own(0, 0)
    for g in range(1, groups):
        pick(g)
        send_own(0, g)

    router_load = load(5, router_hbm, router)
    loads = [
        load(6 + i, source, target)
        for i, (source, target) in enumerate(
            (
                (gain_hbm, gain),
                (wq_hbm, wcat.at[:, pl.ds(0, WIDTH)]),
                (wk_hbm, wcat.at[:, pl.ds(WIDTH, WIDTH)]),
                (wv_hbm, wcat.at[:, pl.ds(2 * WIDTH, WIDTH)]),
                (ck_hbm, ck),
                (cv_hbm, cv),
                (wo_hbm, wo),
            )
        )
    ]
    router_load.wait()
    for s in range(shards):
        lanes = slice(s * WIDTH, (s + 1) * WIDTH)
        wide = jnp.broadcast_to(router[:, lanes].astype(F32), (WIDTH, WIDTH))
        wcat[lanes, 3 * WIDTH :] = jnp.transpose(wide).astype(BF16)
    for g in range(groups):
        step(0, g, 1)
    for g in range(groups):
        pass_rest(g)
    for g in range(groups):
        step(0, g, 2)
    for copy in loads:
        copy.wait()

    steps(0, 0, 3, 4)
    steps(0, 1, 3, 4)
    compute(0)
    steps(0, 2, 3, 4)
    compute(1)
    steps(0, 3, 3, 4)
    compute(2)
    steps(1, 0, 1, 2)
    compute(3)
    steps(1, 1, 1, 2)
    steps(1, 0, 3, 4)
    steps(1, 2, 1, 2)
    steps(1, 1, 3, 4)
    finish(0)
    steps(1, 3, 1, 2)
    steps(1, 2, 3, 4)
    finish(1)
    steps(1, 3, 3, 4)
    finish(2)
    finish(3)

    for g in range(groups):
        drain(0, g)
        drain(1, g)
        next_copy(g).wait()


def body(
    tokens,
    fresh_tokens,
    route_rows,
    block_list,
    norm_gain,
    route_weight,
    w_query,
    w_key,
    w_value,
    w_out,
    cache_keys,
    cache_values,
):
    sections = lax.axis_size("sec")
    shards = lax.axis_size("head")
    chips = shards // 2
    half = chips // 2
    groups, routed = route_rows.shape[1:]
    rows = tokens.shape[0]
    width = shards * WIDTH
    cached = cache_keys.shape[1] // BLOCK
    picked = block_list.shape[2] * BLOCK
    dma = pltpu.SemaphoreType.DMA
    hbm = pl.BlockSpec(memory_space=pl.ANY)
    shifted = pl.pallas_call(
        functools.partial(kernel, sections, chips),
        out_shape=jax.ShapeDtypeStruct((rows, WIDTH), BF16),
        in_specs=[pl.BlockSpec(memory_space=pltpu.SMEM)] + [hbm] * 10,
        out_specs=hbm,
        scratch_shapes=[
            pltpu.VMEM((groups, routed), jnp.int32),
            pltpu.VMEM((1, width), F32),
            pltpu.VMEM((1, width), BF16),
            pltpu.VMEM((rows, WIDTH), BF16),
            pltpu.VMEM((width, 4 * WIDTH), BF16),
            pltpu.VMEM((width, WIDTH), BF16),
            pltpu.VMEM((cached, BLOCK, WIDTH), BF16),
            pltpu.VMEM((cached, BLOCK, WIDTH), BF16),
            pltpu.VMEM((groups, shards, routed, WIDTH), BF16),
            pltpu.VMEM((groups, shards, routed, WIDTH), BF16),
            pltpu.VMEM((routed, width), BF16),
            pltpu.VMEM((2 * routed, picked + groups * routed), F32),
            pltpu.VMEM((groups, routed, WIDTH), BF16),
            pltpu.VMEM((groups, routed, WIDTH), BF16),
            pltpu.VMEM((groups, routed, WIDTH), F32),
            pltpu.VMEM((groups, rows // groups, routed), BF16),
            pltpu.VMEM((rows, WIDTH), BF16),
            pltpu.VMEM((rows, WIDTH), BF16),
            dma((13,)),
            dma((2, groups, 2 * half)),
            dma((2, groups, 2 * half)),
            dma((2, groups, 2 * half)),
            dma((2, groups, 2 * half)),
            dma((groups,)),
            dma((groups,)),
        ],
        compiler_params=pltpu.CompilerParams(
            collective_id=0, has_side_effects=True, vmem_limit_bytes=60 << 20
        ),
    )(
        block_list[0],
        route_rows[0],
        norm_gain,
        route_weight,
        tokens,
        w_query[0],
        w_key[0],
        w_value[0],
        w_out[0],
        cache_keys[0].reshape(cached, BLOCK, WIDTH),
        cache_values[0].reshape(cached, BLOCK, WIDTH),
    )
    return jnp.where(lax.axis_index("sec") == 0, fresh_tokens, shifted)


def solution(mesh):
    in_specs = (
        P("sec", "head"),
        P(None, "head"),
        P("sec", None, None),
        P("sec", None, None),
        P("sec", None),
        P("sec", None),
        P("sec", None, "head"),
        P("sec", None, "head"),
        P("sec", None, "head"),
        P("sec", None, "head"),
        P("sec", None, "head"),
        P("sec", None, "head"),
    )
    return jax.shard_map(
        body, mesh=mesh, in_specs=in_specs, out_specs=P("sec", "head"), check_vma=False
    )
```

```python
import functools

import jax
import jax.numpy as jnp
from jax import lax
from jax.experimental import pallas as pl
from jax.experimental.pallas import tpu as pltpu
from jax.sharding import PartitionSpec as P

HEAD_DIM = 64
BLOCK = 128
WIDTH = 128
MESH = pl.DeviceIdType.MESH
OWN = (1, 2)
ONWARD = {2: (3, 4)}
F32 = jnp.float32
BF16 = jnp.bfloat16


def dot(a, b, dims=((1,), (0,))):
    return lax.dot_general(a, b, (dims, ((), ())), preferred_element_type=F32)


def kernel(
    sections,
    chips,
    blocks_ref,
    route_hbm,
    gain_hbm,
    router_hbm,
    tokens_hbm,
    wq_hbm,
    wk_hbm,
    wv_hbm,
    wo_hbm,
    ck_hbm,
    cv_hbm,
    out_ref,
    route,
    gain,
    router,
    tokens,
    wcat,
    wo,
    ck,
    cv,
    xg,
    ag,
    normed,
    scores,
    queries,
    klocal,
    vlocal,
    gates,
    place,
    passed,
    result,
    load_sem,
    ring_send,
    ring_recv,
    pair_send,
    pair_recv,
    next_send,
    next_recv,
):
    groups, routed = route.shape
    group_rows = tokens.shape[0] // groups
    half = chips // 2
    picked_blocks = blocks_ref.shape[1]
    shards = 2 * chips
    width = shards * WIDTH

    sec = lax.axis_index("sec")
    head = lax.axis_index("head")
    chip = head // 2
    core = head % 2

    def at(off):
        return ((chip + chips + off) % chips) * 2 + core

    pair = chip * 2 + 1 - core
    after = (sec + 1) % sections
    before = (sec + sections - 1) % sections

    def rows_of(g):
        return pl.ds(g * group_rows, group_rows)

    def load(i, source, target):
        copy = pltpu.make_async_copy(source, target, load_sem.at[i])
        copy.start()
        return copy

    route_load = load(0, route_hbm, route)
    token_loads = [
        load(1 + g, tokens_hbm.at[rows_of(g)], tokens.at[rows_of(g)])
        for g in range(groups)
    ]

    barrier = pltpu.get_barrier_semaphore()
    for there in (
        {"head": at(1)},
        {"head": at(-1)},
        {"head": at(2)},
        {"head": at(-2)},
        {"head": pair},
        {"sec": after},
        {"sec": before},
    ):
        pl.semaphore_signal(barrier, inc=1, device_id=there, device_id_type=MESH)

    bufs = (xg, ag)

    def message(p, g, way, reach, dist, slot):
        ref = bufs[p].at[g, slot]
        if reach == half:
            ref = ref.at[pl.ds(way * (routed // 2), routed // 2)]
        i = 2 * (reach - 1) + way
        return pltpu.make_async_remote_copy(
            src_ref=ref,
            dst_ref=ref,
            send_sem=ring_send.at[p, g, i],
            recv_sem=ring_recv.at[p, g, i],
            device_id={"head": at(dist if way == 0 else -dist)},
            device_id_type=MESH,
        )

    def pair_copy(p, g, slot, i):
        ref = bufs[p].at[g, slot]
        return pltpu.make_async_remote_copy(
            src_ref=ref,
            dst_ref=ref,
            send_sem=pair_send.at[p, g, i],
            recv_sem=pair_recv.at[p, g, i],
            device_id={"head": pair},
            device_id_type=MESH,
        )

    def arrived(reach, way):
        return at(-reach if way == 0 else reach)

    def send_own(p, g):
        for reach in OWN:
            for way in (0, 1):
                message(p, g, way, reach, reach, head).start()
        pair_copy(p, g, head, 0).start()

    def step(p, g, reach):
        for way in (0, 1):
            slot = arrived(reach, way)
            message(p, g, way, reach, 1, slot).wait_recv()
            for farther in ONWARD.get(reach, ()):
                message(p, g, way, farther, farther - reach, slot).start()
            if reach < half:
                pair_copy(p, g, slot, 2 * reach - 1 + way).start()
        if reach == half:
            pair_copy(p, g, arrived(reach, 0), 2 * half - 1).start()

    def steps(p, g, *reaches):
        for reach in reaches:
            step(p, g, reach)

    def pair_wait(p, g):
        for i in range(2 * half):
            pair_copy(p, g, pair, i).wait_recv()

    def drain(p, g):
        for reach in range(1, half + 1):
            for way in (0, 1):
                message(p, g, way, reach, 1, head).wait_send()
        for i in range(2 * half):
            pair_copy(p, g, head, i).wait_send()

    def next_copy(g):
        return pltpu.make_async_remote_copy(
            src_ref=result.at[rows_of(g)],
            dst_ref=out_ref.at[rows_of(g)],
            send_sem=next_send.at[g],
            recv_sem=next_recv.at[g],
            device_id={"sec": after},
            device_id_type=MESH,
        )

    def pick(g):
        chosen = route[g : g + 1, :]
        rows = lax.broadcasted_iota(jnp.int32, (group_rows, routed), 0)
        here = jnp.where(rows == chosen, 1.0, 0.0).astype(BF16)
        place[g] = here
        token_loads[g].wait()
        xg[g, head] = dot(here, tokens[rows_of(g), :], ((0,), (0,))).astype(BF16)

    def pass_rest(g):
        used = jnp.max(place[g].astype(F32), axis=1, keepdims=True)
        mine = tokens[rows_of(g), :].astype(F32)
        passed[rows_of(g), :] = jnp.where(used > 0.0, 0.0, mine).astype(BF16)

    def project(g):
        pair_wait(0, g)
        total = jnp.zeros((routed, WIDTH), F32)
        for s in range(shards):
            x = xg[g, s].astype(F32)
            total += x * x
        mean = jnp.sum(total, axis=1, keepdims=True) * (1.0 / width)
        scale = lax.rsqrt(mean + 1e-05)
        gate = jnp.zeros((routed, WIDTH), F32)
        for s in range(shards):
            lanes = slice(s * WIDTH, (s + 1) * WIDTH)
            x = xg[g, s].astype(F32)
            n = (x * scale * gain[:, lanes]).astype(BF16)
            normed[:, lanes] = n
            gate += n.astype(F32) * router[:, lanes].astype(F32)
        y = dot(normed[...], wcat[...])
        logit = jnp.sum(gate, axis=1, keepdims=True)
        gates[g] = jnp.broadcast_to(jax.nn.sigmoid(logit), (routed, WIDTH))
        klocal[g] = y[:, WIDTH : 2 * WIDTH].astype(BF16)
        vlocal[g] = y[:, 2 * WIDTH :].astype(BF16)
        queries[g] = y[:, :WIDTH].astype(BF16)

    def attend(g):
        lane = lax.broadcasted_iota(jnp.int32, (routed, WIDTH), 1)
        first = lane < HEAD_DIM
        qs = queries[g].astype(F32) * 0.125
        both = jnp.concatenate(
            [jnp.where(first, qs, 0.0), jnp.where(first, 0.0, qs)], axis=0
        ).astype(BF16)
        starts = [blocks_ref[g, i] for i in range(picked_blocks)]
        kinds = [(ck, cv, s) for s in starts] + [(klocal, vlocal, c) for c in range(g + 1)]

        r = jnp.broadcast_to(route[g : g + 1, :].astype(F32), (routed, routed))
        visible = r <= jnp.transpose(r)
        visible = jnp.concatenate([visible, visible], axis=0)
        spans = [kinds[i : i + 2] for i in range(0, len(kinds), 2)]
        top = None
        at = 0
        where = []
        for span in spans:
            keys = jnp.concatenate([k[i] for k, _, i in span], axis=0)
            s = dot(both, keys, ((1,), (1,)))
            for j, (k, _, i) in enumerate(span):
                part = s[:, j * BLOCK : (j + 1) * BLOCK]
                if k is klocal and i == g:
                    part = jnp.where(visible, part, -jnp.inf)
                scores[:, at + j * BLOCK : at + (j + 1) * BLOCK] = part
                top = part if top is None else jnp.maximum(top, part)
            where.append((at, BLOCK * len(span)))
            at += BLOCK * len(span)
        high = jnp.max(top, axis=1, keepdims=True)
        total = jnp.zeros((2 * routed, WIDTH), F32)
        acc = jnp.zeros((2 * routed, WIDTH), F32)
        for (at, size), span in zip(where, spans):
            w = jnp.exp(scores[:, at : at + size] - high)
            for j in range(len(span)):
                total += w[:, j * BLOCK : (j + 1) * BLOCK]
            values = jnp.concatenate([v[i] for _, v, i in span], axis=0)
            acc += dot(w.astype(BF16), values)
        denom = jnp.sum(total, axis=1, keepdims=True)
        ratio = acc / denom
        ag[g, head] = jnp.where(first, ratio[:routed], ratio[routed:]).astype(BF16)

    def finish(g):
        pair_wait(1, g)
        attended = jnp.concatenate([ag[g, s] for s in range(shards)], axis=1)
        branch = dot(attended, wo[...])
        updated = (xg[g, head].astype(F32) + gates[g] * branch).astype(BF16)
        moved = dot(place[g], updated)
        rest = passed[rows_of(g), :].astype(F32)
        result[rows_of(g), :] = (moved + rest).astype(BF16)
        next_copy(g).start()

    def answer(g):
        attend(g)
        send_own(1, g)

    route_load.wait()
    pick(0)
    pl.semaphore_wait(barrier, 7)
    send_own(0, 0)
    pick(1)
    send_own(0, 1)
    loads = [
        load(5 + i, source, target)
        for i, (source, target) in enumerate(
            (
                (router_hbm, router),
                (gain_hbm, gain),
                (wq_hbm, wcat.at[:, pl.ds(0, WIDTH)]),
                (wk_hbm, wcat.at[:, pl.ds(WIDTH, WIDTH)]),
                (wv_hbm, wcat.at[:, pl.ds(2 * WIDTH, WIDTH)]),
                (ck_hbm, ck),
                (cv_hbm, cv),
                (wo_hbm, wo),
            )
        )
    ]
    pick(2)
    pick(3)
    steps(0, 0, 1, 2)
    send_own(0, 2)
    steps(0, 1, 1, 2)
    send_own(0, 3)
    steps(0, 0, 3, 4)
    for copy in loads:
        copy.wait()
    project(0)
    steps(0, 2, 1, 2)
    answer(0)
    steps(0, 1, 3, 4)
    project(1)
    steps(0, 3, 1, 2)
    answer(1)
    steps(0, 2, 3, 4)
    project(2)
    steps(1, 0, 1, 2)
    answer(2)
    steps(0, 3, 3, 4)
    project(3)
    steps(1, 1, 1, 2)
    answer(3)
    pass_rest(0)
    pass_rest(1)
    steps(1, 0, 3, 4)
    steps(1, 2, 1, 2)
    steps(1, 1, 3, 4)
    pass_rest(2)
    pass_rest(3)
    finish(0)
    steps(1, 3, 1, 2)
    finish(1)
    steps(1, 2, 3, 4)
    finish(2)
    steps(1, 3, 3, 4)
    finish(3)

    for g in range(groups):
        drain(0, g)
        drain(1, g)
        next_copy(g).wait()


def body(
    tokens,
    fresh_tokens,
    route_rows,
    block_list,
    norm_gain,
    route_weight,
    w_query,
    w_key,
    w_value,
    w_out,
    cache_keys,
    cache_values,
):
    sections = lax.axis_size("sec")
    shards = lax.axis_size("head")
    chips = shards // 2
    half = chips // 2
    groups, routed = route_rows.shape[1:]
    rows = tokens.shape[0]
    width = shards * WIDTH
    cached = cache_keys.shape[1] // BLOCK
    picked = block_list.shape[2] * BLOCK
    dma = pltpu.SemaphoreType.DMA
    hbm = pl.BlockSpec(memory_space=pl.ANY)
    shifted = pl.pallas_call(
        functools.partial(kernel, sections, chips),
        out_shape=jax.ShapeDtypeStruct((rows, WIDTH), BF16),
        in_specs=[pl.BlockSpec(memory_space=pltpu.SMEM)] + [hbm] * 10,
        out_specs=hbm,
        scratch_shapes=[
            pltpu.VMEM((groups, routed), jnp.int32),
            pltpu.VMEM((1, width), F32),
            pltpu.VMEM((1, width), BF16),
            pltpu.VMEM((rows, WIDTH), BF16),
            pltpu.VMEM((width, 3 * WIDTH), BF16),
            pltpu.VMEM((width, WIDTH), BF16),
            pltpu.VMEM((cached, BLOCK, WIDTH), BF16),
            pltpu.VMEM((cached, BLOCK, WIDTH), BF16),
            pltpu.VMEM((groups, shards, routed, WIDTH), BF16),
            pltpu.VMEM((groups, shards, routed, WIDTH), BF16),
            pltpu.VMEM((routed, width), BF16),
            pltpu.VMEM((2 * routed, picked + groups * routed), F32),
            pltpu.VMEM((groups, routed, WIDTH), BF16),
            pltpu.VMEM((groups, routed, WIDTH), BF16),
            pltpu.VMEM((groups, routed, WIDTH), BF16),
            pltpu.VMEM((groups, routed, WIDTH), F32),
            pltpu.VMEM((groups, rows // groups, routed), BF16),
            pltpu.VMEM((rows, WIDTH), BF16),
            pltpu.VMEM((rows, WIDTH), BF16),
            dma((13,)),
            dma((2, groups, 2 * half)),
            dma((2, groups, 2 * half)),
            dma((2, groups, 2 * half)),
            dma((2, groups, 2 * half)),
            dma((groups,)),
            dma((groups,)),
        ],
        compiler_params=pltpu.CompilerParams(
            collective_id=0, has_side_effects=True, vmem_limit_bytes=60 << 20
        ),
    )(
        block_list[0],
        route_rows[0],
        norm_gain,
        route_weight,
        tokens,
        w_query[0],
        w_key[0],
        w_value[0],
        w_out[0],
        cache_keys[0].reshape(cached, BLOCK, WIDTH),
        cache_values[0].reshape(cached, BLOCK, WIDTH),
    )
    return jnp.where(lax.axis_index("sec") == 0, fresh_tokens, shifted)


def solution(mesh):
    in_specs = (
        P("sec", "head"),
        P(None, "head"),
        P("sec", None, None),
        P("sec", None, None),
        P("sec", None),
        P("sec", None),
        P("sec", None, "head"),
        P("sec", None, "head"),
        P("sec", None, "head"),
        P("sec", None, "head"),
        P("sec", None, "head"),
        P("sec", None, "head"),
    )
    return jax.shard_map(
        body, mesh=mesh, in_specs=in_specs, out_specs=P("sec", "head"), check_vma=False
    )
```
